32 devices in a mesh: vel: 16 (over z, x, core), box: 2 (over y).
Axes of the slice: x: 2, y: 2, z: 4, core: 2. Of those that a mesh axis runs over, the one named last changes fastest.
Arguments:
- distribution: float32 [4096, 3, 3, 3, 2, 128], P('vel', None, None, None, 'box'), may hold values from -2.5 to 2.5, as said below
- collision_rate: float32 [2, 128], P('box'), may hold values from 1 to 10
Outputs:
- advanced: float32 [4096, 3, 3, 3, 2, 128], P('vel', None, None, None, 'box')
The draws below stay inside these ranges and needn't reach their ends.
Inputs may be any that keep to these rules, and one draw needn't show every extreme that they name: `distribution`: coefficient (0,0,0) is positive for every box and velocity; every other coefficient is at most coefficient (0,0,0) of the same box and velocity in magnitude.
All inputs are finite; a program needn't handle non-finite values.
Results may differ from the reference program's by a relative error of at most 0.0003.
Values sent between devices are 32-bit elements; how exact they have to be, the bound alone decides.
A program may use at most 64 MiB of HBM per device.

```python
import math
import jax
import jax.numpy as jnp
from jax import lax

VPD = 16
MODES = 3
NY = 8
NZ = 16
NX = 2
NYZ = 128


def grid_speeds():
    spacing = 8.0 / VPD
    index = jnp.arange(VPD ** 3, dtype=jnp.int32)

    def centre(number):
        return -4.0 + (number.astype(jnp.float32) + 0.5) * spacing
    return (centre(index // (VPD * VPD)), centre(index // VPD % VPD), centre(index % VPD))


def smooth_field(key):
    phases = jax.random.uniform(key, (3,), jnp.float32, 0.0, 2.0 * jnp.pi)
    along_x = jnp.sin(2.0 * jnp.pi * jnp.arange(NX, dtype=jnp.float32) / NX + phases[0])
    along_y = jnp.sin(2.0 * jnp.pi * jnp.arange(NY, dtype=jnp.float32) / NY + phases[1])
    along_z = jnp.sin(2.0 * jnp.pi * jnp.arange(NZ, dtype=jnp.float32) / NZ + phases[2])
    total = along_x[:, None, None] + along_y[None, :, None] + along_z[None, None, :]
    return (total / 3.0).reshape(NX, NY * NZ)


def draw_distribution(key, part):
    shape = (VPD ** 3, MODES, MODES, MODES, NX, NY * NZ)
    salt = 20
    density = 4.0 * 8.0 ** (0.5 * (smooth_field(jax.random.fold_in(key, salt + 1)) + 1.0))
    flow_x = smooth_field(jax.random.fold_in(key, salt + 2))
    flow_y = smooth_field(jax.random.fold_in(key, salt + 3))
    flow_z = smooth_field(jax.random.fold_in(key, salt + 4))
    temper = 4.0 ** (0.5 * (smooth_field(jax.random.fold_in(key, salt + 5)) + 1.0))
    speed_x, speed_y, speed_z = grid_speeds()
    offset_x = speed_x[:, None, None] - flow_x[None]
    offset_y = speed_y[:, None, None] - flow_y[None]
    offset_z = speed_z[:, None, None] - flow_z[None]
    spread = offset_x * offset_x + offset_y * offset_y + offset_z * offset_z
    maxwell = density[None] * (2.0 * jnp.pi * temper[None]) ** (-1.5) * jnp.exp(-spread / (2.0 * temper[None]))
    noise_key = jax.random.fold_in(key, salt + 6)
    noise = jax.random.uniform(noise_key, maxwell.shape, jnp.float32, -1.0, 1.0)
    base = maxwell * (1.0 + 0.2 * noise)
    higher = 0.2 * jax.random.truncated_normal(jax.random.fold_in(key, salt + 7), -5.0, 5.0, shape, jnp.float32)
    higher = higher * base[:, None, None, None]
    modes = jnp.arange(MODES ** 3, dtype=jnp.int32).reshape(1, MODES, MODES, MODES, 1, 1)
    return jnp.where(modes == 0, base[:, None, None, None], higher)


def block_levels(own_key, shape, split, least, high):
    gain, own = 1.0, jax.random.fold_in(own_key, 6)
    for position, blocks in split:
        steps = jnp.exp(jax.random.uniform(jax.random.fold_in(own, position), (blocks,), jnp.float32, least / len(split), high / len(split)))
        gain = gain * jnp.repeat(steps, shape[position] // blocks).reshape([-1 if axis == position else 1 for axis in range(len(shape))])
    return gain


def setup_inputs(seed: int = 0) -> dict:
    seeds = jax.random.split(jax.random.key(seed), 3)
    distribution = draw_distribution(jax.random.fold_in(seeds[2], 71), 0)
    collision_rate = jnp.clip(jnp.exp(math.log(10.0) - 2.3025851 * jax.random.uniform(seeds[1], (NX, NYZ), jnp.float32) ** block_levels(seeds[1], (NX, NYZ), ((0, 2),), -0.2, 0.2)), 1.0, 10.0)
    return {"distribution": distribution, "collision_rate": collision_rate}


SPEED_LIMIT = 4.0
TIME_STEP = 0.02
HIGHEST = lax.Precision.HIGHEST


def speeds(index):
    spacing = 2.0 * SPEED_LIMIT / VPD
    first = index // (VPD * VPD)
    second = (index // VPD) % VPD
    third = index % VPD

    def centre(number):
        return -SPEED_LIMIT + (number.astype(jnp.float32) + 0.5) * spacing

    return centre(first), centre(second), centre(third)


def moment_table(index):
    speed_x, speed_y, speed_z = speeds(index)
    weight = (2.0 * SPEED_LIMIT / VPD) ** 3
    energy = 0.5 * (speed_x * speed_x + speed_y * speed_y + speed_z * speed_z)
    return weight * jnp.stack([jnp.ones_like(speed_x), speed_x, speed_y, speed_z, energy])


def primitives(totals):
    density = totals[0]
    flow = totals[1:4] / density
    temper = (2.0 * totals[4] / density - jnp.sum(flow * flow, axis=0)) / 3.0
    return jnp.concatenate([density[None], flow, temper[None]], axis=0)


def face_traces(field, axis):
    first = jnp.take(field, 0, axis)
    second = jnp.take(field, 1, axis)
    third = jnp.take(field, 2, axis)
    return first + second + third, first - second + third


def transport(field, axis, speed, upper, lower, upper_prev, lower_next):
    positive = speed > 0
    upper_flux = jnp.where(positive, upper, lower_next)
    lower_flux = jnp.where(positive, upper_prev, lower)
    first = jnp.take(field, 0, axis)
    second = jnp.take(field, 1, axis)
    rate_zero = speed * (lower_flux - upper_flux)
    rate_one = 3.0 * speed * (2.0 * first - upper_flux - lower_flux)
    rate_two = 5.0 * speed * (2.0 * second - upper_flux + lower_flux)
    return jnp.stack([rate_zero, rate_one, rate_two], axis)


def z_previous(values):
    cells = jnp.arange(values.shape[-1], dtype=jnp.int32) % NZ
    return jnp.where(cells == 0, jnp.roll(values, 1 - NZ, -1), jnp.roll(values, 1, -1))


def z_following(values):
    cells = jnp.arange(values.shape[-1], dtype=jnp.int32) % NZ
    return jnp.where(cells == NZ - 1, jnp.roll(values, NZ - 1, -1), jnp.roll(values, -1, -1))


def block_rate(field, index, states, collision_rate, upper_prev, lower_next):
    speed_x, speed_y, speed_z = speeds(index)
    shaped = (-1, 1, 1, 1, 1)
    upper, lower = face_traces(field, 1)
    total = transport(field, 1, speed_x.reshape(shaped), upper, lower, upper_prev, lower_next)
    upper, lower = face_traces(field, 2)
    total = total + transport(field, 2, speed_y.reshape(shaped), upper, lower,
                              jnp.roll(upper, NZ, -1), jnp.roll(lower, -NZ, -1))
    upper, lower = face_traces(field, 3)
    total = total + transport(field, 3, speed_z.reshape(shaped), upper, lower,
                              z_previous(upper), z_following(lower))
    density = states[0]
    temper = states[4]
    offset_x = speed_x[:, None, None] - states[1]
    offset_y = speed_y[:, None, None] - states[2]
    offset_z = speed_z[:, None, None] - states[3]
    spread = offset_x * offset_x + offset_y * offset_y + offset_z * offset_z
    maxwell = density * (2.0 * jnp.pi * temper) ** (-1.5) * jnp.exp(-spread / (2.0 * temper))
    total = total - collision_rate * field
    return total.at[:, 0, 0, 0].add(collision_rate * maxwell)


def section_rate(field, collision_rate):
    count = field.shape[0]
    index = jnp.arange(count, dtype=jnp.int32)
    base = field[:, 0, 0, 0].reshape(count, -1)
    totals = jnp.dot(moment_table(index), base, precision=HIGHEST)
    states = primitives(totals).reshape((5,) + field.shape[4:])
    blocks = max(count // 256, 1)
    width = count // blocks

    def one_block(pair):
        piece, start = pair
        upper, lower = face_traces(piece, 1)
        local_index = start + jnp.arange(width, dtype=jnp.int32)
        return block_rate(piece, local_index, states, collision_rate,
                          jnp.roll(upper, 1, 3), jnp.roll(lower, -1, 3))

    pieces = field.reshape((blocks, width) + field.shape[1:])
    starts = jnp.arange(blocks, dtype=jnp.int32) * width
    rates = lax.map(one_block, (pieces, starts))
    return rates.reshape(field.shape)


def reference(distribution, collision_rate):
    middle = distribution + TIME_STEP * section_rate(distribution, collision_rate)
    final_rate = section_rate(middle, collision_rate)
    return 0.5 * distribution + 0.5 * (middle + TIME_STEP * final_rate)
```

```python
import functools

import jax
import jax.numpy as jnp
from jax import lax
from jax.experimental import pallas as pl
from jax.experimental.pallas import tpu as pltpu
from jax.sharding import PartitionSpec as P

VPD = 16
NZ = 16
MODES = 3

SPEED_LIMIT = 4.0
TIME_STEP = 0.02
SPACING = 2.0 * SPEED_LIMIT / VPD
CUBE = MODES ** 3
FACE = MODES ** 2
SUB = 8
HALVES = VPD // SUB
MESH = pl.DeviceIdType.MESH


def centre(number):
    return -SPEED_LIMIT + (number.astype(jnp.float32) + 0.5) * SPACING


def line_modes(dim, number):
    stride = MODES ** (2 - dim)
    first = number // stride * stride * MODES + number % stride
    return [first + a * stride for a in range(MODES)]


def kernel(nvel, nbox, count, f_hbm, nu_ref, out_hbm, f_v, o_v, mid, trace, halo,
           slots, in_sem, out_sem, x_send, x_recv, m_send, m_recv):
    lanes = f_v.shape[-1]
    chunks = count // VPD
    rows = VPD * CUBE
    me_vel = lax.axis_index("vel")
    me_box = lax.axis_index("box")
    start = me_vel * count
    first = start // (VPD * VPD)
    positive = first >= VPD // 2
    ahead = lax.rem(me_box + 1, nbox)
    behind = lax.rem(me_box + nbox - 1, nbox)
    target = jnp.where(positive, ahead, behind)
    source = jnp.where(positive, behind, ahead)

    def load_copy(c):
        part = pl.ds(pl.multiple_of(c * rows, SUB), rows)
        return pltpu.make_async_copy(f_hbm.at[part], f_v.at[part], in_sem.at[c])

    def store_copy(c):
        part = pl.ds(pl.multiple_of(c * rows, SUB), rows)
        return pltpu.make_async_copy(o_v.at[part], out_hbm.at[part], out_sem.at[c])

    def halo_copy(section, c):
        return pltpu.make_async_remote_copy(
            src_ref=trace.at[section, c], dst_ref=halo.at[section, c],
            send_sem=x_send.at[section, c], recv_sem=x_recv.at[section, c],
            device_id={"box": target}, device_id_type=MESH)

    def moment_copy(section, k, slot):
        return pltpu.make_async_remote_copy(
            src_ref=slots.at[section, slot], dst_ref=slots.at[section, slot],
            send_sem=m_send.at[section, k], recv_sem=m_recv.at[section, slot],
            device_id={"vel": lax.rem(me_vel + k, nvel)}, device_id_type=MESH)

    def each(low, high, body):
        def step(i, carry):
            body(i)
            return carry
        lax.fori_loop(low, high, step, 0)

    each(0, chunks, lambda c: load_copy(c).start())

    barrier = pltpu.get_barrier_semaphore()
    pl.semaphore_signal(barrier, inc=1, device_id={"box": source}, device_id_type=MESH)
    each(1, nvel, lambda k: pl.semaphore_signal(
        barrier, inc=1, device_id={"vel": lax.rem(me_vel + k, nvel)}, device_id_type=MESH))
    pl.semaphore_wait(barrier, nvel)

    speed_x = centre(first)
    sign_x = jnp.where(positive, 1.0, -1.0)
    row = lax.broadcasted_iota(jnp.int32, (SUB, lanes), 0)
    cell = lax.broadcasted_iota(jnp.int32, (SUB, lanes), 1) % NZ
    speeds_z = [centre(row + h * SUB) for h in range(HALVES)]

    def z_neighbour(values, h):
        if 2 * h >= HALVES:
            return jnp.where(cell == 0, pltpu.roll(values, lanes + 1 - NZ, 1), pltpu.roll(values, 1, 1))
        return jnp.where(cell == NZ - 1, pltpu.roll(values, NZ - 1, 1), pltpu.roll(values, lanes - 1, 1))

    def field(c, h):
        base = (c * VPD + h * SUB) * CUBE
        return [f_v[pl.ds(base + m, SUB, stride=CUBE), :] for m in range(CUBE)]

    def put_trace(section, c, h, values):
        for q in range(FACE):
            m0, m1, m2 = (values[m] for m in line_modes(0, q))
            trace[section, c, h * FACE + q] = m0 + m2 + sign_x * m1

    def gathered(sums, c, h, base):
        speed_y = centre(lax.rem(start // VPD + c, VPD))
        speed_z = speeds_z[h]
        zero, along_y, along_z, square = sums
        return (zero + base, along_y + speed_y * base, along_z + speed_z * base,
                square + (speed_y * speed_y + speed_z * speed_z) * base)

    def exchange(section, sums):
        zero, along_y, along_z, square = (jnp.sum(s, axis=0, keepdims=True) for s in sums)
        weight = SPACING ** 3
        terms = (zero, speed_x * zero, along_y, along_z, 0.5 * (speed_x * speed_x * zero + square))
        tile = jnp.zeros((SUB, lanes), jnp.float32)
        for r, term in enumerate(terms):
            tile = jnp.where(row == r, weight * term, tile)
        slots[section, me_vel] = tile
        each(1, nvel, lambda k: moment_copy(section, k, me_vel).start())

    def states(section):
        each(1, nvel, lambda k: moment_copy(section, k, lax.rem(me_vel + k, nvel)).wait_recv())
        total = lax.fori_loop(1, nvel, lambda k, s: s + slots[section, k], slots[section, 0])
        density = total[0:1]
        flow = [total[r:r + 1] / density for r in (1, 2, 3)]
        square = flow[0] * flow[0] + flow[1] * flow[1] + flow[2] * flow[2]
        temper = (2.0 * total[4:5] / density - square) / 3.0
        root = 1.0 / jnp.sqrt(2.0 * jnp.pi * temper)
        nu = TIME_STEP * nu_ref[...]
        wide = lambda v: jnp.broadcast_to(v, (SUB, lanes))
        return (wide(nu * density * (root * root * root)), wide(flow[0]), wide(flow[1]), wide(flow[2]),
                wide(-0.5 / temper))

    keep = jnp.broadcast_to(1.0 - TIME_STEP * nu_ref[...], (SUB, lanes))

    def stepped(section, c, h, m, state):
        second = lax.rem(start // VPD + c, VPD)
        speed_y = centre(second)
        up_y = second >= VPD // 2
        sign_y = jnp.where(up_y, 1.0, -1.0)
        shift_y = jnp.where(up_y, NZ, lanes - NZ)
        speed_z = speeds_z[h]
        up_z = 2 * h >= HALVES
        acc = [keep * v for v in m]

        def transport(dim, speed, size, own, other):
            a = TIME_STEP * size
            w3 = (3.0 * TIME_STEP) * speed
            w10 = (10.0 * TIME_STEP) * speed
            for q in range(FACE):
                i0, i1, i2 = line_modes(dim, q)
                mine = own(q, i0, i1, i2)
                near = other(q, mine)
                jump = a * (near - mine)
                acc[i0] = acc[i0] + jump
                acc[i1] = acc[i1] + w3 * ((m[i0] + m[i0]) - (mine + near))
                acc[i2] = acc[i2] + (w10 * m[i1] + 5.0 * jump)

        transport(2, speed_z, speed_z if up_z else -speed_z,
                  lambda q, i0, i1, i2: m[i0] + m[i2] + m[i1] if up_z else m[i0] + m[i2] - m[i1],
                  lambda q, mine: z_neighbour(mine, h))
        transport(1, speed_y, sign_y * speed_y,
                  lambda q, i0, i1, i2: m[i0] + m[i2] + sign_y * m[i1],
                  lambda q, mine: pltpu.roll(mine, shift_y, 1))
        transport(0, speed_x, sign_x * speed_x,
                  lambda q, i0, i1, i2: trace[section, c, h * FACE + q],
                  lambda q, mine: halo[section, c, h * FACE + q])
        scale, flow_x, flow_y, flow_z, narrow = state
        off_x = speed_x - flow_x
        off_y = speed_y - flow_y
        off_z = speed_z - flow_z
        spread = off_x * off_x + off_y * off_y + off_z * off_z
        acc[0] = acc[0] + scale * jnp.exp(spread * narrow)
        return acc

    zeros = (jnp.zeros((SUB, lanes), jnp.float32),) * 4

    def opening(c, sums):
        load_copy(c).wait()
        for h in range(HALVES):
            values = field(c, h)
            put_trace(0, c, h, values)
            sums = gathered(sums, c, h, values[0])
        halo_copy(0, c).start()
        return sums

    exchange(0, lax.fori_loop(0, chunks, opening, zeros))
    state_one = states(0)

    def section_one(c, sums):
        halo_copy(0, c).wait_recv()
        for h in range(HALVES):
            acc = stepped(0, c, h, field(c, h), state_one)
            for m in range(CUBE):
                mid[c * HALVES + h, m] = acc[m]
            put_trace(1, c, h, acc)
            sums = gathered(sums, c, h, acc[0])
        halo_copy(1, c).start()
        return sums

    exchange(1, lax.fori_loop(0, chunks, section_one, zeros))
    state_two = states(1)

    def section_two(c):
        halo_copy(1, c).wait_recv()
        for h in range(HALVES):
            values = [mid[c * HALVES + h, m] for m in range(CUBE)]
            acc = stepped(1, c, h, values, state_two)
            base = (c * VPD + h * SUB) * CUBE
            for m in range(CUBE):
                place = pl.ds(base + m, SUB, stride=CUBE)
                o_v[place, :] = 0.5 * f_v[place, :] + 0.5 * acc[m]
        store_copy(c).start()

    each(0, chunks, section_two)

    for section in range(2):
        each(0, chunks, lambda c: halo_copy(section, c).wait_send())
        each(1, nvel, lambda k: moment_copy(section, k, me_vel).wait_send())
    each(0, chunks, lambda c: store_copy(c).wait())


def shards(nvel, nbox, distribution, collision_rate):
    count = distribution.shape[0]
    lanes = distribution.shape[-1]
    assert (VPD * VPD) % count == 0 and count % VPD == 0
    assert distribution.shape[4] == 1
    chunks = count // VPD
    total = count * CUBE
    f32 = jnp.float32
    out = pl.pallas_call(
        functools.partial(kernel, nvel, nbox, count),
        out_shape=jax.ShapeDtypeStruct((total, lanes), f32),
        in_specs=[pl.BlockSpec(memory_space=pl.ANY), pl.BlockSpec(memory_space=pltpu.VMEM)],
        out_specs=pl.BlockSpec(memory_space=pl.ANY),
        scratch_shapes=[
            pltpu.VMEM((total, lanes), f32),
            pltpu.VMEM((total, lanes), f32),
            pltpu.VMEM((chunks * HALVES, CUBE, SUB, lanes), f32),
            pltpu.VMEM((2, chunks, HALVES * FACE, SUB, lanes), f32),
            pltpu.VMEM((2, chunks, HALVES * FACE, SUB, lanes), f32),
            pltpu.VMEM((2, nvel, SUB, lanes), f32),
            pltpu.SemaphoreType.DMA((chunks,)),
            pltpu.SemaphoreType.DMA((chunks,)),
            pltpu.SemaphoreType.DMA((2, chunks)),
            pltpu.SemaphoreType.DMA((2, chunks)),
            pltpu.SemaphoreType.DMA((2, nvel)),
            pltpu.SemaphoreType.DMA((2, nvel)),
        ],
        compiler_params=pltpu.CompilerParams(
            collective_id=0, has_side_effects=True, vmem_limit_bytes=40 * 2 ** 20),
        cost_estimate=pl.CostEstimate(flops=total * lanes * 80, bytes_accessed=total * lanes * 8,
                                      transcendentals=2 * count * lanes),
    )(distribution.reshape(total, lanes), collision_rate)
    return out.reshape(distribution.shape)


def solution(mesh):
    return jax.shard_map(
        functools.partial(shards, mesh.shape["vel"], mesh.shape["box"]),
        mesh=mesh,
        in_specs=(P("vel", None, None, None, "box", None), P("box", None)),
        out_specs=P("vel", None, None, None, "box", None),
        check_vma=False,
    )
```

```python
import functools

import jax
import jax.numpy as jnp
from jax import lax
from jax.experimental import pallas as pl
from jax.experimental.pallas import tpu as pltpu
from jax.sharding import PartitionSpec as P

VPD = 16
NZ = 16
MODES = 3

SPEED_LIMIT = 4.0
TIME_STEP = 0.02
SPACING = 2.0 * SPEED_LIMIT / VPD
CUBE = MODES ** 3
FACE = MODES ** 2
SUB = 8
HALVES = VPD // SUB
EARLY = 2
MESH = pl.DeviceIdType.MESH


def centre(number):
    return -SPEED_LIMIT + (number.astype(jnp.float32) + 0.5) * SPACING


def line_modes(dim, number):
    stride = MODES ** (2 - dim)
    first = number // stride * stride * MODES + number % stride
    return [first + a * stride for a in range(MODES)]


def kernel(nvel, nbox, count, f_hbm, nu_ref, o_v, f_v, mid, trace, halo,
           slots, in_sem, x_send, x_recv, m_send, m_recv):
    lanes = f_v.shape[-1]
    chunks = count // VPD
    rows = VPD * CUBE
    me_vel = lax.axis_index("vel")
    me_box = lax.axis_index("box")
    start = me_vel * count
    first = start // (VPD * VPD)
    positive = first >= VPD // 2
    ahead = lax.rem(me_box + 1, nbox)
    behind = lax.rem(me_box + nbox - 1, nbox)
    target = jnp.where(positive, ahead, behind)
    source = jnp.where(positive, behind, ahead)

    def load_copy(c):
        part = pl.ds(pl.multiple_of(c * rows, SUB), rows)
        return pltpu.make_async_copy(f_hbm.at[part], f_v.at[part], in_sem.at[c])

    def halo_copy(section, c):
        s = section * chunks + c
        return pltpu.make_async_remote_copy(
            src_ref=trace.at[s], dst_ref=halo.at[s], send_sem=x_send.at[s], recv_sem=x_recv.at[s],
            device_id={"box": target}, device_id_type=MESH)

    def moment_copy(section, k, slot):
        return pltpu.make_async_remote_copy(
            src_ref=slots.at[section, slot], dst_ref=slots.at[section, slot],
            send_sem=m_send.at[section, k], recv_sem=m_recv.at[section, slot],
            device_id={"vel": lax.rem(me_vel + k, nvel)}, device_id_type=MESH)

    def each(low, high, body):
        def step(i, carry):
            body(i)
            return carry
        lax.fori_loop(low, high, step, 0)

    each(0, chunks, lambda c: load_copy(c).start())

    barrier = pltpu.get_barrier_semaphore()
    pl.semaphore_signal(barrier, inc=1, device_id={"box": source}, device_id_type=MESH)
    each(1, nvel, lambda k: pl.semaphore_signal(
        barrier, inc=1, device_id={"vel": lax.rem(me_vel + k, nvel)}, device_id_type=MESH))

    speed_x = centre(first)
    sign_x = jnp.where(positive, 1.0, -1.0)
    row = lax.broadcasted_iota(jnp.int32, (SUB, lanes), 0)
    cell = lax.broadcasted_iota(jnp.int32, (SUB, lanes), 1) % NZ
    speeds_z = [centre(row + h * SUB) for h in range(HALVES)]

    def z_neighbour(values, h):
        if 2 * h >= HALVES:
            return jnp.where(cell == 0, pltpu.roll(values, lanes + 1 - NZ, 1), pltpu.roll(values, 1, 1))
        return jnp.where(cell == NZ - 1, pltpu.roll(values, NZ - 1, 1), pltpu.roll(values, lanes - 1, 1))

    def field(c, h):
        base = (c * VPD + h * SUB) * CUBE
        return [f_v[pl.ds(base + m, SUB, stride=CUBE), :] for m in range(CUBE)]

    def put_trace(section, c, h, values):
        for q in range(FACE):
            m0, m1, m2 = (values[m] for m in line_modes(0, q))
            trace[section * chunks + c, h * FACE + q] = m0 + m2 + sign_x * m1

    def gathered(sums, c, h, base):
        speed_y = centre(lax.rem(start // VPD + c, VPD))
        speed_z = speeds_z[h]
        zero, along_y, along_z, square = sums
        return (zero + base, along_y + speed_y * base, along_z + speed_z * base,
                square + (speed_y * speed_y + speed_z * speed_z) * base)

    def exchange(section, sums):
        zero, along_y, along_z, square = (jnp.sum(s, axis=0, keepdims=True) for s in sums)
        weight = SPACING ** 3
        terms = (zero, speed_x * zero, along_y, along_z, 0.5 * (speed_x * speed_x * zero + square))
        tile = jnp.zeros((SUB, lanes), jnp.float32)
        for r, term in enumerate(terms):
            tile = jnp.where(row == r, weight * term, tile)
        slots[section, me_vel] = tile
        each(1, nvel, lambda k: moment_copy(section, k, me_vel).start())

    def states(section):
        each(1, nvel, lambda k: moment_copy(section, k, lax.rem(me_vel + k, nvel)).wait_recv())
        total = lax.fori_loop(1, nvel, lambda k, s: s + slots[section, k], slots[section, 0])
        density = total[0:1]
        flow = [total[r:r + 1] / density for r in (1, 2, 3)]
        square = flow[0] * flow[0] + flow[1] * flow[1] + flow[2] * flow[2]
        temper = (2.0 * total[4:5] / density - square) / 3.0
        root = 1.0 / jnp.sqrt(2.0 * jnp.pi * temper)
        nu = TIME_STEP * nu_ref[...]
        wide = lambda v: jnp.broadcast_to(v, (SUB, lanes))
        return (wide(nu * density * (root * root * root)), wide(flow[0]), wide(flow[1]), wide(flow[2]),
                wide(-0.5 / temper))

    keep = jnp.broadcast_to(1.0 - TIME_STEP * nu_ref[...], (SUB, lanes))

    def stepped(section, c, h, m, state):
        second = lax.rem(start // VPD + c, VPD)
        speed_y = centre(second)
        up_y = second >= VPD // 2
        sign_y = jnp.where(up_y, 1.0, -1.0)
        shift_y = jnp.where(up_y, NZ, lanes - NZ)
        speed_z = speeds_z[h]
        up_z = 2 * h >= HALVES
        acc = [keep * v for v in m]

        def transport(dim, speed, size, own, other):
            a = TIME_STEP * size
            w3 = (3.0 * TIME_STEP) * speed
            w10 = (10.0 * TIME_STEP) * speed
            for q in range(FACE):
                i0, i1, i2 = line_modes(dim, q)
                mine = own(q, i0, i1, i2)
                near = other(q, mine)
                jump = a * (near - mine)
                acc[i0] = acc[i0] + jump
                acc[i1] = acc[i1] + w3 * ((m[i0] + m[i0]) - (mine + near))
                acc[i2] = acc[i2] + (w10 * m[i1] + 5.0 * jump)

        transport(2, speed_z, speed_z if up_z else -speed_z,
                  lambda q, i0, i1, i2: m[i0] + m[i2] + m[i1] if up_z else m[i0] + m[i2] - m[i1],
                  lambda q, mine: z_neighbour(mine, h))
        transport(1, speed_y, sign_y * speed_y,
                  lambda q, i0, i1, i2: m[i0] + m[i2] + sign_y * m[i1],
                  lambda q, mine: pltpu.roll(mine, shift_y, 1))
        transport(0, speed_x, sign_x * speed_x,
                  lambda q, i0, i1, i2: trace[section * chunks + c, h * FACE + q],
                  lambda q, mine: halo[section * chunks + c, h * FACE + q])
        scale, flow_x, flow_y, flow_z, narrow = state
        off_x = speed_x - flow_x
        off_y = speed_y - flow_y
        off_z = speed_z - flow_z
        spread = off_x * off_x + off_y * off_y + off_z * off_z
        acc[0] = acc[0] + scale * jnp.exp(spread * narrow)
        return acc

    zeros = (jnp.zeros((SUB, lanes), jnp.float32),) * 4

    def opening(c, sums):
        load_copy(c).wait()
        for h in range(HALVES):
            values = field(c, h)
            put_trace(0, c, h, values)
            sums = gathered(sums, c, h, values[0])
        return sums

    def opening_sent(c, sums):
        sums = opening(c, sums)
        halo_copy(0, c).start()
        return sums

    ready = min(EARLY, chunks)
    sums = lax.fori_loop(0, ready, opening, zeros)
    pl.semaphore_wait(barrier, nvel)
    each(0, ready, lambda c: halo_copy(0, c).start())
    exchange(0, lax.fori_loop(ready, chunks, opening_sent, sums))
    state_one = states(0)

    def section_one(c, sums):
        halo_copy(0, c).wait_recv()
        for h in range(HALVES):
            acc = stepped(0, c, h, field(c, h), state_one)
            for m in range(CUBE):
                mid[c * HALVES + h, m] = acc[m]
            put_trace(1, c, h, acc)
            sums = gathered(sums, c, h, acc[0])
        halo_copy(1, c).start()
        return sums

    exchange(1, lax.fori_loop(0, chunks, section_one, zeros))
    state_two = states(1)

    def section_two(c):
        halo_copy(1, c).wait_recv()
        for h in range(HALVES):
            values = [mid[c * HALVES + h, m] for m in range(CUBE)]
            acc = stepped(1, c, h, values, state_two)
            base = (c * VPD + h * SUB) * CUBE
            for m in range(CUBE):
                place = pl.ds(base + m, SUB, stride=CUBE)
                o_v[place, :] = 0.5 * f_v[place, :] + 0.5 * acc[m]

    each(0, chunks, section_two)

    for section in range(2):
        each(0, chunks, lambda c: halo_copy(section, c).wait_send())
        each(1, nvel, lambda k: moment_copy(section, k, me_vel).wait_send())


def shards(nvel, nbox, distribution, collision_rate):
    count = distribution.shape[0]
    lanes = distribution.shape[-1]
    assert (VPD * VPD) % count == 0 and count % VPD == 0
    assert distribution.shape[4] == 1
    chunks = count // VPD
    total = count * CUBE
    f32 = jnp.float32
    out = pl.pallas_call(
        functools.partial(kernel, nvel, nbox, count),
        out_shape=jax.ShapeDtypeStruct((total, lanes), f32),
        in_specs=[pl.BlockSpec(memory_space=pl.ANY), pl.BlockSpec(memory_space=pltpu.VMEM)],
        out_specs=pl.BlockSpec(memory_space=pltpu.VMEM),
        scratch_shapes=[
            pltpu.VMEM((total, lanes), f32),
            pltpu.VMEM((chunks * HALVES, CUBE, SUB, lanes), f32),
            pltpu.VMEM((2 * chunks, HALVES * FACE, SUB, lanes), f32),
            pltpu.VMEM((2 * chunks, HALVES * FACE, SUB, lanes), f32),
            pltpu.VMEM((2, nvel, SUB, lanes), f32),
            pltpu.SemaphoreType.DMA((chunks,)),
            pltpu.SemaphoreType.DMA((2 * chunks,)),
            pltpu.SemaphoreType.DMA((2 * chunks,)),
            pltpu.SemaphoreType.DMA((2, nvel)),
            pltpu.SemaphoreType.DMA((2, nvel)),
        ],
        compiler_params=pltpu.CompilerParams(
            collective_id=0, has_side_effects=True, vmem_limit_bytes=50 * 2 ** 20),
        cost_estimate=pl.CostEstimate(flops=total * lanes * 80, bytes_accessed=total * lanes * 8,
                                      transcendentals=2 * count * lanes),
    )(distribution.reshape(total, lanes), collision_rate)
    return out.reshape(distribution.shape)


def solution(mesh):
    return jax.shard_map(
        functools.partial(shards, mesh.shape["vel"], mesh.shape["box"]),
        mesh=mesh,
        in_specs=(P("vel", None, None, None, "box", None), P("box", None)),
        out_specs=P("vel", None, None, None, "box", None),
        check_vma=False,
    )
```
